32 devices in a mesh: grp: 2 (over x), seq: 8 (over z, y), tp: 2 (over core).
Axes of the slice: x: 2, y: 2, z: 4, core: 2. Of those that a mesh axis runs over, the one named last changes fastest.
Arguments:
- queries: bfloat16 [2048, 5120], P(('grp', 'seq'), 'tp'), parts along dimension 0, may hold values from -80 to 80
- key_heads: bfloat16 [2048, 1024], P(('grp', 'seq'), 'tp'), parts along dimension 0, may hold values from -6 to 6
- values: bfloat16 [2048, 1024], P(('grp', 'seq'), 'tp'), parts along dimension 0, may hold values from -6 to 6
- residual: bfloat16 [2048, 5120], P(('grp', 'seq'), 'tp'), parts along dimension 0, may hold values from -4 to 4
- doc_start: int32 [2048], P(('grp', 'seq')), parts along dimension 0, may hold values from 0 to 1023, as said below
- norm_gain: bfloat16 [5120], P('tp'), may hold values from 0.5 to 1.5
- router: bfloat16 [5120, 4], P('tp'), may hold values from -0.078125 to 0.078125
- expert_id: int32 [2048], P(('grp', 'seq')), parts along dimension 0, may hold values from 0 to 3, as said below
- slot_index: int32 [2048], P(('grp', 'seq')), parts along dimension 0, may hold values from 0 to 47, as said below
- gate_weight: bfloat16 [5120, 16384], P('tp', 'seq'), may hold values from -0.078125 to 0.078125
- up_weight: bfloat16 [5120, 16384], P('tp', 'seq'), may hold values from -0.078125 to 0.078125
- down_weight: bfloat16 [16384, 5120], P('seq', 'tp'), may hold values from -0.09375 to 0.09375
Outputs:
- layer_out: bfloat16 [2048, 5120], P(('grp', 'seq'), 'tp'), parts along dimension 0
The draws below stay inside these ranges and needn't reach their ends.
There are 2 independent parts, one for each index of `grp`. The reference program is written for one: setup_inputs(seed, part) draws one part's arguments, and reference() takes and returns one part's arrays. A program takes and returns all parts, laid end to end along the dimension named above; an argument that names none is the same for every part. Nothing has to cross between parts.
Inputs may be any that keep to these rules, and one draw needn't show every extreme that they name: Document starts never fall along the sequence and doc_start[t] <= t. `expert_id`: among the tokens of one index of seq no expert is named more than 48 times, and one expert is named exactly 48 times in every such block. `slot_index`: tokens of one index of seq that name the same expert have distinct slots.
All inputs are finite; a program needn't handle non-finite values.
Results may differ from the reference program's by a relative error of at most 0.008.
Values may be sent and summed in bfloat16 or wider, within the bound.
A program may use at most 128 MiB of HBM per device.

```python
import math
import jax
import jax.numpy as jnp
from jax import lax

D = 5120
QH = 40
KVH = 8
HD = 128
FF = 4096
EXPERTS = 4
TOK_DEV = 128
TOKENS = 1024
STRETCH = 512
SPAN = 2
FEW = 2048
CAP = 48


def route_table(key):
    block_count = TOKENS // TOK_DEV
    hot_expert = jax.random.randint(jax.random.fold_in(key, 7), (), 0, EXPERTS).astype(jnp.int32)

    def one_block(number):
        block_key = jax.random.fold_in(key, number + 1000)
        others = jax.random.permutation(jax.random.fold_in(block_key, 1), (EXPERTS - 1) * CAP)[:TOK_DEV - CAP].astype(jnp.int32)
        other_expert = others // CAP
        other_expert = other_expert + (other_expert >= hot_expert).astype(jnp.int32)
        named = jnp.concatenate([jnp.full((CAP,), hot_expert, jnp.int32), other_expert])
        places = jnp.concatenate([jnp.arange(CAP, dtype=jnp.int32), others % CAP])
        order = jax.random.permutation(jax.random.fold_in(block_key, 2), TOK_DEV)
        return (named[order], places[order])
    named_all, placed_all = jax.vmap(one_block)(jnp.arange(block_count, dtype=jnp.int32))
    return (named_all.reshape(-1), placed_all.reshape(-1))


def key_table(key):
    base = jax.random.normal(jax.random.fold_in(key, 11), (TOKENS, KVH, HD), jnp.float32)
    return jnp.clip(base, -6.0, 6.0)


def draw_expert_id(key, part):
    named, placed = route_table(key)
    return named


def draw_slot_index(key, part):
    named, placed = route_table(key)
    return placed


def draw_key_heads(key, part):
    base = key_table(key)
    return base.reshape(TOKENS, KVH * HD).astype(jnp.bfloat16)


def draw_queries(key, part):
    key = jax.random.fold_in(key, 6)
    fresh = jnp.clip(jax.random.normal(key, (TOKENS, QH, HD), jnp.float32) * 1.8, -10.0, 10.0)
    return fresh.reshape(TOKENS, QH * HD).astype(jnp.bfloat16)


def draw_doc_start(key, part):
    key = jax.random.fold_in(key, 8)
    position = jnp.arange(TOKENS, dtype=jnp.int32)
    starts = (jax.random.randint(key, (TOKENS,), 0, 2 * TOK_DEV) == 0) | (position == 0)
    return lax.cummax(jnp.where(starts, position, jnp.zeros_like(position)), axis=0)


def level_of(key, extent, split, low, top_value):
    def one(axis_at, blocks):
        draws = jax.random.uniform(jax.random.fold_in(jax.random.fold_in(key, 6), axis_at), (blocks,), jnp.float32, low / len(split), top_value / len(split))
        return jnp.repeat(jnp.exp(draws), extent[axis_at] // blocks).reshape((-1,) + (1,) * (len(extent) - axis_at - 1))

    loudness = one(*split[0])
    for cut in split[1:]:
        loudness = loudness * one(*cut)
    return loudness


def gaussian(key, shape, spread, bound, split=(), held_as=jnp.bfloat16):
    result = spread * jax.random.normal(key, shape, jnp.float32)
    if split:
        result = result * level_of(key, shape, split, -0.22, 0.18)
    return jnp.clip(result, -bound, bound).astype(held_as)


def setup_inputs(seed: int = 0, part: int = 0) -> dict:
    seeds = jax.random.split(jax.random.key(seed), 13)
    part_splits = jax.random.split(jax.random.fold_in(seeds[12], part), 13)
    return {
        "queries": draw_queries(jax.random.fold_in(jax.random.fold_in(seeds[12], part), 71), part),
        "key_heads": draw_key_heads(jax.random.fold_in(jax.random.fold_in(seeds[12], part), 71), part),
        "values": gaussian(part_splits[2], (TOKENS, KVH * HD), 1.0, 6.0, ((0, 8), (1, 2))),
        "residual": gaussian(part_splits[3], (TOKENS, D), 0.5, 4.0, ((0, 8), (1, 2))),
        "doc_start": draw_doc_start(jax.random.fold_in(jax.random.fold_in(seeds[12], part), 71), part),
        "norm_gain": jnp.clip(0.5 + 1.0 * jax.random.uniform(seeds[5], (D,), jnp.float32) ** level_of(seeds[5], (D,), ((0, 2),), -0.2, 0.2), 0.5, 1.5).astype(jnp.bfloat16),
        "router": gaussian(seeds[6], (D, EXPERTS), D ** -0.5, 0.078125, ((0, 2),)),
        "expert_id": draw_expert_id(jax.random.fold_in(jax.random.fold_in(seeds[12], part), 71), part),
        "slot_index": draw_slot_index(jax.random.fold_in(jax.random.fold_in(seeds[12], part), 71), part),
        "gate_weight": gaussian(seeds[9], (D, EXPERTS * FF), D ** -0.5, 0.078125, ((0, 2), (1, 8))),
        "up_weight": gaussian(seeds[10], (D, EXPERTS * FF), D ** -0.5, 0.078125, ((0, 2), (1, 8))),
        "down_weight": gaussian(seeds[11], (EXPERTS * FF, D), FF ** -0.5, 0.09375, ((0, 8), (1, 2))),
    }


def reference(queries, key_heads, values, residual, doc_start, norm_gain, router, expert_id, slot_index, gate_weight, up_weight, down_weight):
    per_group = QH // KVH
    stretch_count = TOKENS // STRETCH
    score_scale = 1.0 / math.sqrt(HD)
    query_all = queries.reshape(stretch_count, STRETCH, KVH, per_group, HD)
    key_all = key_heads.reshape(stretch_count, STRETCH, KVH, HD)
    value_all = values.reshape(stretch_count, STRETCH, KVH, HD)
    start_all = doc_start.reshape(stretch_count, STRETCH)

    def one_stretch(inputs):
        query_part, key_part, value_part, start_part, number = inputs
        scores = jnp.einsum('tkgd,skd->kgts', query_part.astype(jnp.float32), key_part.astype(jnp.float32)) * score_scale
        position = jnp.arange(STRETCH, dtype=jnp.int32)
        global_pos = number * STRETCH + position
        allowed = (position[None, :] <= position[:, None]) & (global_pos[None, :] >= start_part[:, None])
        masked = jnp.where(allowed, scores, -jnp.inf)
        largest = lax.optimization_barrier(jnp.max(masked, axis=-1, keepdims=True))
        exponent = jnp.exp(masked - largest)
        denominator = lax.optimization_barrier(jnp.sum(exponent, axis=-1, keepdims=True))
        probabilities = exponent.astype(jnp.bfloat16)
        attended = jnp.einsum('kgts,skd->tkgd', probabilities.astype(jnp.float32), value_part.astype(jnp.float32))
        attended = attended / jnp.transpose(denominator, (2, 0, 1, 3))
        return attended.reshape(STRETCH, D)
    attention = lax.map(one_stretch, (query_all, key_all, value_all, start_all, jnp.arange(stretch_count, dtype=jnp.int32)))
    attention = attention.reshape(TOKENS, D)
    hidden_state = (residual.astype(jnp.float32) + attention).astype(jnp.bfloat16)
    gained = (hidden_state.astype(jnp.float32) * norm_gain.astype(jnp.float32)).astype(jnp.bfloat16)
    inverse = lax.rsqrt(lax.optimization_barrier(jnp.sum(jnp.square(hidden_state.astype(jnp.float32)), axis=1)) / D + 1e-05)
    logits = inverse[:, None] * jnp.dot(gained, router, preferred_element_type=jnp.float32)
    picked = jnp.take_along_axis(logits, expert_id[:, None].astype(jnp.int32), axis=1)[:, 0]
    factor = inverse * jax.nn.sigmoid(picked)
    expert_in = (gained.astype(jnp.float32) * factor[:, None]).astype(jnp.bfloat16)
    block_count = TOKENS // TOK_DEV
    block_number = jnp.arange(TOKENS, dtype=jnp.int32) // TOK_DEV
    place = (block_number * EXPERTS + expert_id.astype(jnp.int32)) * CAP + slot_index.astype(jnp.int32)
    buffer = jnp.zeros((block_count * EXPERTS * CAP, D), jnp.bfloat16).at[place].set(expert_in)
    buffer = buffer.reshape(block_count, EXPERTS, CAP, D).transpose(1, 0, 2, 3).reshape(EXPERTS, block_count * CAP, D)
    gate_all = gate_weight.reshape(D, EXPERTS, FF).transpose(1, 0, 2)
    up_all = up_weight.reshape(D, EXPERTS, FF).transpose(1, 0, 2)
    down_all = down_weight.reshape(EXPERTS, SPAN, FEW, D)

    def serve_one(inputs):
        rows, gate_one, up_one, down_one = inputs
        gate = jnp.dot(rows, gate_one, preferred_element_type=jnp.float32)
        upward = jnp.dot(rows, up_one, preferred_element_type=jnp.float32)
        activated = (jax.nn.silu(gate) * upward).astype(jnp.bfloat16)
        sliced = activated.reshape(rows.shape[0], SPAN, FEW).astype(jnp.float32)
        pieces = jnp.einsum('rjf,jfd->rjd', sliced, down_one.astype(jnp.float32))
        rounded = lax.optimization_barrier(pieces.astype(jnp.bfloat16))
        return lax.optimization_barrier(jnp.sum(rounded.astype(jnp.float32), axis=1))
    produced = lax.map(serve_one, (buffer, gate_all, up_all, down_all))
    unrolled = produced.reshape(EXPERTS, block_count, CAP, D).transpose(1, 0, 2, 3).reshape(-1, D)
    expert_out = unrolled[place]
    return (hidden_state.astype(jnp.float32) + expert_out).astype(jnp.bfloat16)
```

```python
import functools
import math

import jax
import jax.numpy as jnp
from jax import lax
from jax.experimental import pallas as pl
from jax.experimental.pallas import tpu as pltpu
from jax.sharding import PartitionSpec as P

D = 5120
QH = 40
KVH = 8
HD = 128
STRETCH_DEVS = 4


def shifted(array, axis, by):
    devices = lax.axis_size(axis)
    pairs = [(i, i + by) for i in range(devices) if 0 <= i + by < devices]
    return lax.ppermute(array, axis, pairs)


MESH = pl.DeviceIdType.MESH
VMEM_LIMIT = 60 * 1024 * 1024


def peer_of(expert, step):
    if step == 0:
        return expert
    if step == 1:
        return expert + 1 - 2 * (expert % 2)
    if step == 2:
        return (expert + 2) % 4
    return 3 - expert


def expert_kernel(
    span,
    cap,
    ein,
    sel,
    sel_t,
    hid,
    gate_hbm,
    up_hbm,
    down_hbm,
    out,
    gate_w,
    up_w,
    down_w,
    outgoing,
    rows_in,
    own_part,
    part_send,
    part_recv,
    act,
    piece,
    piece_recv,
    back,
    returned,
    w_sem,
    disp_s,
    disp_r,
    fwd_s,
    fwd_r,
    tp_s,
    tp_r,
    y_s,
    y_r,
    z_s,
    z_r,
):
    experts = 4
    me = lax.axis_index("seq")
    core = lax.axis_index("tp")
    e = me // span
    j = me % span
    feats = ein.shape[1]
    hidden = gate_w.shape[1]
    ft = 512
    ht = min(512, hidden)

    weights = [
        pltpu.make_async_copy(src, dst, w_sem.at[i])
        for i, (src, dst) in enumerate(((gate_hbm, gate_w), (up_hbm, up_w), (down_hbm, down_w)))
    ]
    for copy in weights:
        copy.start()

    barrier = pltpu.get_barrier_semaphore()
    for step in range(1, experts):
        pl.semaphore_signal(
            barrier, inc=1, device_id={"seq": peer_of(e, step) * span + j}, device_id_type=MESH
        )
    for d in range(1, span):
        pl.semaphore_signal(
            barrier, inc=1, device_id={"seq": e * span + (j + d) % span}, device_id_type=MESH
        )
    pl.semaphore_signal(barrier, inc=1, device_id={"tp": 1 - core}, device_id_type=MESH)

    def slots(number):
        return pl.ds(pl.multiple_of(number * cap, 16), cap)

    @pl.loop(0, feats // ft)
    def _(c):
        cols = pl.ds(pl.multiple_of(c * ft, ft), ft)
        outgoing[:, cols] = jnp.dot(
            sel[...], ein[:, cols], preferred_element_type=jnp.float32
        ).astype(jnp.bfloat16)

    pl.semaphore_wait(barrier, experts - 1 + span)

    def disp(step):
        return pltpu.make_async_remote_copy(
            src_ref=outgoing.at[slots(peer_of(e, step))],
            dst_ref=rows_in.at[step, slots(j)],
            send_sem=disp_s.at[step],
            recv_sem=disp_r.at[step],
            device_id={"seq": peer_of(e, step) * span + j},
            device_id_type=MESH,
        )

    def fwd(step, d):
        src = outgoing.at[slots(e)] if step == 0 else rows_in.at[step, slots(j)]
        return pltpu.make_async_remote_copy(
            src_ref=src,
            dst_ref=rows_in.at[step, slots(j)],
            send_sem=fwd_s.at[step, d],
            recv_sem=fwd_r.at[step, d],
            device_id={"seq": e * span + (j + d) % span},
            device_id_type=MESH,
        )

    def tp_copy(step):
        return pltpu.make_async_remote_copy(
            src_ref=part_send.at[step],
            dst_ref=part_recv.at[step],
            send_sem=tp_s.at[step],
            recv_sem=tp_r.at[step],
            device_id={"tp": 1 - core},
            device_id_type=MESH,
        )

    def y_copy(step, d):
        return pltpu.make_async_remote_copy(
            src_ref=piece.at[step, slots((j + d) % span)],
            dst_ref=piece_recv.at[step, d - 1],
            send_sem=y_s.at[step, d],
            recv_sem=y_r.at[step, d],
            device_id={"seq": e * span + (j + d) % span},
            device_id_type=MESH,
        )

    def z_copy(step):
        return pltpu.make_async_remote_copy(
            src_ref=back.at[step],
            dst_ref=returned.at[slots(e)],
            send_sem=z_s.at[step],
            recv_sem=z_r.at[step],
            device_id={"seq": peer_of(e, step) * span + j},
            device_id_type=MESH,
        )

    def forward(step):
        if step > 0:
            disp(step).wait_recv()
        for d in range(1, span):
            fwd(step, d).start()

    def gate_up(step):
        for d in range(1, span):
            fwd(step, d).wait_recv()

        @pl.loop(0, hidden // ht)
        def _(c):
            for weight, base in ((gate_w, 0), (up_w, hidden)):
                cols = pl.ds(pl.multiple_of(c * ht, ht), ht)
                to = pl.ds(pl.multiple_of(base + c * ht, ht), ht)
                part = jnp.dot(
                    rows_in[step], weight[:, cols], preferred_element_type=jnp.float32
                )
                own_part[step, :, to] = part
                part_send[step, :, to] = part.astype(jnp.bfloat16)

        tp_copy(step).start()

    def down(step):
        tp_copy(step).wait_recv()

        @pl.loop(0, hidden // ht)
        def _(c):
            cols = pl.ds(pl.multiple_of(c * ht, ht), ht)
            ups = pl.ds(pl.multiple_of(hidden + c * ht, ht), ht)
            gate = own_part[step, :, cols] + part_recv[step, :, cols].astype(jnp.float32)
            up = own_part[step, :, ups] + part_recv[step, :, ups].astype(jnp.float32)
            act[:, cols] = (jax.nn.silu(gate) * up).astype(jnp.bfloat16)

        @pl.loop(0, feats // ft)
        def _(c):
            cols = pl.ds(pl.multiple_of(c * ft, ft), ft)
            piece[step, :, cols] = jnp.dot(
                act[...], down_w[:, cols], preferred_element_type=jnp.float32
            ).astype(jnp.bfloat16)

        for d in range(1, span):
            y_copy(step, d).start()

    def give_back(step):
        for d in range(1, span):
            y_copy(step, d).wait_recv()

        @pl.loop(0, feats // ft)
        def _(c):
            cols = pl.ds(pl.multiple_of(c * ft, ft), ft)
            total = piece[step, slots(j), cols].astype(jnp.float32)
            for d in range(1, span):
                total += piece_recv[step, d - 1, :, cols].astype(jnp.float32)
            if step == 0:
                returned[slots(e), cols] = total.astype(jnp.bfloat16)
            else:
                back[step, :, cols] = total.astype(jnp.bfloat16)

        if step > 0:
            z_copy(step).start()

    for step in (3, 2, 1):
        disp(step).start()
    forward(0)
    rows_in[0, slots(j)] = outgoing[slots(e)]
    forward(1)
    weights[0].wait()
    weights[1].wait()
    gate_up(0)
    forward(2)
    gate_up(1)
    forward(3)
    weights[2].wait()
    down(0)
    down(1)
    gate_up(2)
    give_back(1)
    gate_up(3)
    down(2)
    give_back(0)
    down(3)
    give_back(2)
    give_back(3)
    for step in range(1, experts):
        z_copy(step).wait_recv()

    @pl.loop(0, feats // ft)
    def _(c):
        cols = pl.ds(pl.multiple_of(c * ft, ft), ft)
        picked = jnp.dot(sel_t[...], returned[:, cols], preferred_element_type=jnp.float32)
        out[:, cols] = (hid[:, cols].astype(jnp.float32) + picked).astype(jnp.bfloat16)

    for step in range(experts):
        if step > 0:
            disp(step).wait_send()
            z_copy(step).wait_send()
        tp_copy(step).wait_send()
        for d in range(1, span):
            fwd(step, d).wait_send()
            y_copy(step, d).wait_send()


def expert_block(expert_in, select, hidden_state, gate_weight, up_weight, down_weight, cap, span):
    tokens, feats = expert_in.shape
    hidden = gate_weight.shape[1]
    experts = select.shape[0] // cap
    rows = span * cap
    bf16 = jnp.bfloat16
    vmem = pl.BlockSpec(memory_space=pltpu.VMEM)
    hbm = pl.BlockSpec(memory_space=pl.ANY)
    dma = pltpu.SemaphoreType.DMA
    return pl.pallas_call(
        functools.partial(expert_kernel, span, cap),
        out_shape=jax.ShapeDtypeStruct((tokens, feats), bf16),
        in_specs=[vmem] * 4 + [hbm] * 3,
        out_specs=vmem,
        scratch_shapes=[
            pltpu.VMEM((feats, hidden), bf16),
            pltpu.VMEM((feats, hidden), bf16),
            pltpu.VMEM((hidden, feats), bf16),
            pltpu.VMEM((experts * cap, feats), bf16),
            pltpu.VMEM((experts, rows, feats), bf16),
            pltpu.VMEM((experts, rows, 2 * hidden), jnp.float32),
            pltpu.VMEM((experts, rows, 2 * hidden), bf16),
            pltpu.VMEM((experts, rows, 2 * hidden), bf16),
            pltpu.VMEM((rows, hidden), bf16),
            pltpu.VMEM((experts, rows, feats), bf16),
            pltpu.VMEM((experts, span - 1, cap, feats), bf16),
            pltpu.VMEM((experts, cap, feats), bf16),
            pltpu.VMEM((experts * cap, feats), bf16),
            dma((3,)),
            dma((experts,)),
            dma((experts,)),
            dma((experts, span)),
            dma((experts, span)),
            dma((experts,)),
            dma((experts,)),
            dma((experts, span)),
            dma((experts, span)),
            dma((experts,)),
            dma((experts,)),
        ],
        compiler_params=pltpu.CompilerParams(
            collective_id=0, has_side_effects=True, vmem_limit_bytes=VMEM_LIMIT
        ),
        name="experts",
    )(
        expert_in,
        select,
        select.T,
        hidden_state,
        gate_weight,
        up_weight,
        down_weight,
    )


def on_device(
    queries,
    key_heads,
    values,
    residual,
    doc_start,
    norm_gain,
    router,
    expert_id,
    slot_index,
    gate_weight,
    up_weight,
    down_weight,
):
    tokens_dev = queries.shape[0]
    per_group = QH // KVH
    kv_local = key_heads.shape[1] // HD
    stretch_len = STRETCH_DEVS * tokens_dev
    score_scale = 1.0 / math.sqrt(HD)
    device = lax.axis_index("seq")
    own_block = (key_heads, values)
    blocks = []
    carried = own_block
    for distance in range(1, STRETCH_DEVS):
        carried = shifted((carried[0], carried[1]), "seq", 1)
        blocks.append(carried)
    ordered = blocks[::-1] + [own_block]
    key_all = jnp.concatenate([piece[0] for piece in ordered], 0).reshape(-1, kv_local, HD)
    value_all = jnp.concatenate([piece[1] for piece in ordered], 0).reshape(-1, kv_local, HD)
    query_view = queries.reshape(tokens_dev, kv_local, per_group, HD)
    scores = (
        jnp.einsum("tkgd,skd->kgts", query_view, key_all, preferred_element_type=jnp.float32)
        * score_scale
    )
    query_pos = device * tokens_dev + jnp.arange(tokens_dev, dtype=jnp.int32)
    key_pos = (device - (STRETCH_DEVS - 1)) * tokens_dev + jnp.arange(
        STRETCH_DEVS * tokens_dev, dtype=jnp.int32
    )
    allowed = (
        (key_pos[None, :] <= query_pos[:, None])
        & (key_pos[None, :] // stretch_len == query_pos[:, None] // stretch_len)
        & (key_pos[None, :] >= doc_start[:, None])
    )
    masked = jnp.where(allowed, scores, -jnp.inf)
    largest = jnp.max(masked, axis=-1, keepdims=True)
    exponent = jnp.exp(masked - largest)
    denominator = jnp.sum(exponent, axis=-1, keepdims=True)
    probabilities = exponent.astype(jnp.bfloat16)
    attended = jnp.einsum(
        "kgts,skd->tkgd", probabilities, value_all, preferred_element_type=jnp.float32
    )
    attended = (attended / jnp.transpose(denominator, (2, 0, 1, 3))).reshape(tokens_dev, -1)
    hidden_state = (residual.astype(jnp.float32) + attended).astype(jnp.bfloat16)
    gained = (hidden_state.astype(jnp.float32) * norm_gain.astype(jnp.float32)).astype(jnp.bfloat16)
    square_part = jnp.sum(jnp.square(hidden_state.astype(jnp.float32)), axis=1)
    logit_part = jnp.dot(gained, router, preferred_element_type=jnp.float32)
    square_sum, logit_sum = lax.psum((square_part, logit_part), "tp")
    inverse = lax.rsqrt(square_sum / D + 1e-05)
    experts_all = router.shape[1]
    chosen = expert_id[:, None] == jnp.arange(experts_all, dtype=jnp.int32)[None, :]
    picked = jnp.sum(jnp.where(chosen, inverse[:, None] * logit_sum, 0.0), axis=1)
    factor = inverse * jax.nn.sigmoid(picked)
    expert_in = (gained.astype(jnp.float32) * factor[:, None]).astype(jnp.bfloat16)
    capacity = 3 * tokens_dev // (2 * experts_all)
    slices_per_expert = lax.axis_size("seq") // experts_all
    place = expert_id * capacity + slot_index
    select = (
        jnp.arange(experts_all * capacity, dtype=jnp.int32)[:, None] == place[None, :]
    ).astype(jnp.bfloat16)
    return expert_block(
        expert_in,
        select,
        hidden_state,
        gate_weight,
        up_weight,
        down_weight,
        capacity,
        slices_per_expert,
    )


def solution(mesh):
    return jax.shard_map(
        on_device,
        mesh=mesh,
        in_specs=(
            P(("grp", "seq"), "tp"),
            P(("grp", "seq"), "tp"),
            P(("grp", "seq"), "tp"),
            P(("grp", "seq"), "tp"),
            P(("grp", "seq")),
            P("tp"),
            P("tp", None),
            P(("grp", "seq")),
            P(("grp", "seq")),
            P("tp", "seq"),
            P("tp", "seq"),
            P("seq", "tp"),
        ),
        out_specs=P(("grp", "seq"), "tp"),
        check_vma=False,
    )
```

```python
import functools
import math

import jax
import jax.numpy as jnp
from jax import lax
from jax.experimental import pallas as pl
from jax.experimental.pallas import tpu as pltpu
from jax.sharding import PartitionSpec as P

D = 5120
QH = 40
KVH = 8
HD = 128
STRETCH_DEVS = 4


MESH = pl.DeviceIdType.MESH
VMEM_LIMIT = 60 * 1024 * 1024


def peer_of(expert, step):
    if step == 0:
        return expert
    if step == 1:
        return expert + 1 - 2 * (expert % 2)
    if step == 2:
        return (expert + 2) % 4
    return 3 - expert


def layer_kernel(
    span,
    cap,
    queries,
    keys,
    values,
    residual,
    ids,
    gain,
    router,
    gate_hbm,
    up_hbm,
    down_hbm,
    out,
    gate_w,
    up_w,
    down_w,
    key_all,
    value_all,
    bias,
    probs,
    totals,
    hid,
    gained,
    stat,
    stat_recv,
    outgoing,
    rows_in,
    own_part,
    part_send,
    part_recv,
    act,
    piece,
    piece_recv,
    back,
    returned,
    w_sem,
    k_s,
    k_r,
    v_s,
    v_r,
    st_s,
    st_r,
    disp_s,
    disp_r,
    fwd_s,
    fwd_r,
    tp_s,
    tp_r,
    y_s,
    y_r,
    z_s,
    z_r,
):
    experts = 4
    me = lax.axis_index("seq")
    core = lax.axis_index("tp")
    e = me // span
    j = me % span
    feats = queries.shape[1]
    tokens = queries.shape[0]
    hidden = gate_w.shape[1]
    ft = 512
    ht = min(512, hidden)

    weights = [
        pltpu.make_async_copy(src, dst, w_sem.at[i])
        for i, (src, dst) in enumerate(((gate_hbm, gate_w), (up_hbm, up_w), (down_hbm, down_w)))
    ]
    for copy in weights:
        copy.start()

    barrier = pltpu.get_barrier_semaphore()
    for step in range(1, experts):
        pl.semaphore_signal(
            barrier, inc=1, device_id={"seq": peer_of(e, step) * span + j}, device_id_type=MESH
        )
    for d in range(1, span):
        pl.semaphore_signal(
            barrier, inc=1, device_id={"seq": e * span + (j + d) % span}, device_id_type=MESH
        )
    pl.semaphore_signal(barrier, inc=1, device_id={"tp": 1 - core}, device_id_type=MESH)
    place = me % STRETCH_DEVS
    for d in range(1, STRETCH_DEVS):
        pl.semaphore_signal(
            barrier,
            inc=1,
            device_id={"seq": me - place + (place + d) % STRETCH_DEVS},
            device_id_type=MESH,
        )

    def slots(number):
        return pl.ds(pl.multiple_of(number * cap, 16), cap)

    f32 = jnp.float32
    key_all[0] = keys[...]
    value_all[0] = values[...]

    across = lax.broadcasted_iota(jnp.int32, (tokens, tokens), 1)
    below = lax.broadcasted_iota(jnp.int32, (tokens, tokens), 0)

    def column(row):
        spread = jnp.broadcast_to(ids[row : row + 1, :].astype(f32), (tokens, tokens))
        return jnp.sum(jnp.where(across == below, spread, 0.0), axis=1, keepdims=True).astype(
            jnp.int32
        )

    start_col = column(0)
    expert_col = column(1)
    place_col = column(2)
    query_pos = me * tokens + below
    for d in range(STRETCH_DEVS):
        key_pos = (me - d) * tokens + across
        allowed = (
            (key_pos <= query_pos) & (key_pos >= start_col) & (key_pos >= (me - place) * tokens)
        )
        bias[:, d * tokens : (d + 1) * tokens] = jnp.where(allowed, 0.0, -jnp.inf)

    pl.semaphore_wait(barrier, experts - 1 + span + STRETCH_DEVS - 1)

    def kv_copy(src, dst, send, recv, d):
        return pltpu.make_async_remote_copy(
            src_ref=src,
            dst_ref=dst.at[d],
            send_sem=send.at[d],
            recv_sem=recv.at[d],
            device_id={"seq": me + d},
            device_id_type=MESH,
        )

    for src, dst, send, recv in (
        (keys, key_all, k_s, k_r),
        (values, value_all, v_s, v_r),
    ):
        for d in range(STRETCH_DEVS - 1, 0, -1):

            @pl.when(place + d < STRETCH_DEVS)
            def _():
                kv_copy(src, dst, send, recv, d).start()

            @pl.when(place < d)
            def _():
                dst[d] = jnp.zeros_like(src)

    for d in range(1, STRETCH_DEVS):

        @pl.when(place >= d)
        def _():
            kv_copy(keys, key_all, k_s, k_r, d).wait_recv()

    kv_heads = keys.shape[1] // HD
    per_group = QH // KVH
    scale = math.log2(math.e) / math.sqrt(HD)

    @pl.loop(0, kv_heads)
    def _(g):
        kcols = pl.ds(pl.multiple_of(g * HD, HD), HD)
        key_block = key_all[:, :, kcols].reshape(STRETCH_DEVS * tokens, HD)
        for r in range(per_group):
            h = g * per_group + r
            cols = pl.ds(pl.multiple_of(h * HD, HD), HD)
            scores = lax.dot_general(
                queries[:, cols], key_block, (((1,), (1,)), ((), ())), preferred_element_type=f32
            )
            masked = scores + bias[...]
            largest = jnp.max(masked, axis=1, keepdims=True)
            expo = jnp.exp2((masked - largest) * scale)
            totals[h] = jnp.broadcast_to(jnp.sum(expo, axis=1, keepdims=True), (tokens, HD))
            probs[h] = expo.astype(jnp.bfloat16)

    for d in range(1, STRETCH_DEVS):

        @pl.when(place >= d)
        def _():
            kv_copy(values, value_all, v_s, v_r, d).wait_recv()

    stat[...] = jnp.zeros_like(stat)

    @pl.loop(0, kv_heads)
    def _(g):
        kcols = pl.ds(pl.multiple_of(g * HD, HD), HD)
        value_block = value_all[:, :, kcols].reshape(STRETCH_DEVS * tokens, HD)
        for r in range(per_group):
            h = g * per_group + r
            cols = pl.ds(pl.multiple_of(h * HD, HD), HD)
            attended = jnp.dot(probs[h], value_block, preferred_element_type=f32) / totals[h]
            state = (residual[:, cols].astype(f32) + attended).astype(jnp.bfloat16)
            hid[:, cols] = state
            wide = state.astype(f32)
            gained[:, cols] = (wide * gain[:, cols].astype(f32)).astype(jnp.bfloat16)
            stat[...] += wide * wide

    square = jnp.sum(stat[...], axis=1, keepdims=True)
    logits = jnp.dot(gained[...], router[...], preferred_element_type=f32)
    lane = lax.broadcasted_iota(jnp.int32, (tokens, experts), 1)
    picked = jnp.sum(jnp.where(lane == expert_col, logits, 0.0), axis=1, keepdims=True)
    stat[...] = jnp.where(across == 0, picked, square)
    stat_copy = pltpu.make_async_remote_copy(
        src_ref=stat,
        dst_ref=stat_recv,
        send_sem=st_s.at[0],
        recv_sem=st_r.at[0],
        device_id={"tp": 1 - core},
        device_id_type=MESH,
    )
    stat_copy.start()
    slot_row = lax.broadcasted_iota(jnp.int32, (experts * cap, tokens), 0)
    slot_lane = lax.broadcasted_iota(jnp.int32, (tokens, experts * cap), 1)
    sel = jnp.where(slot_row == ids[2:3, :], 1.0, 0.0).astype(jnp.bfloat16)
    sel_t = jnp.where(slot_lane == place_col, 1.0, 0.0).astype(jnp.bfloat16)
    stat_copy.wait_recv()
    both = stat[...] + stat_recv[...]
    inverse = lax.rsqrt(both[:, 1:2] / D + 1e-05)
    factor = inverse * jax.nn.sigmoid(inverse * both[:, 0:1])

    @pl.loop(0, feats // ft)
    def _(c):
        cols = pl.ds(pl.multiple_of(c * ft, ft), ft)
        expert_in = (gained[:, cols].astype(f32) * factor).astype(jnp.bfloat16)
        outgoing[:, cols] = jnp.dot(sel, expert_in, preferred_element_type=f32).astype(
            jnp.bfloat16
        )

    def disp(step):
        return pltpu.make_async_remote_copy(
            src_ref=outgoing.at[slots(peer_of(e, step))],
            dst_ref=rows_in.at[step, slots(j)],
            send_sem=disp_s.at[step],
            recv_sem=disp_r.at[step],
            device_id={"seq": peer_of(e, step) * span + j},
            device_id_type=MESH,
        )

    def fwd(step, d):
        src = outgoing.at[slots(e)] if step == 0 else rows_in.at[step, slots(j)]
        return pltpu.make_async_remote_copy(
            src_ref=src,
            dst_ref=rows_in.at[step, slots(j)],
            send_sem=fwd_s.at[step, d],
            recv_sem=fwd_r.at[step, d],
            device_id={"seq": e * span + (j + d) % span},
            device_id_type=MESH,
        )

    def tp_copy(step):
        return pltpu.make_async_remote_copy(
            src_ref=part_send.at[step],
            dst_ref=part_recv.at[step],
            send_sem=tp_s.at[step],
            recv_sem=tp_r.at[step],
            device_id={"tp": 1 - core},
            device_id_type=MESH,
        )

    def y_copy(step, d):
        return pltpu.make_async_remote_copy(
            src_ref=piece.at[step, slots((j + d) % span)],
            dst_ref=piece_recv.at[step, d - 1],
            send_sem=y_s.at[step, d],
            recv_sem=y_r.at[step, d],
            device_id={"seq": e * span + (j + d) % span},
            device_id_type=MESH,
        )

    def z_copy(step):
        return pltpu.make_async_remote_copy(
            src_ref=back.at[step],
            dst_ref=returned.at[slots(e)],
            send_sem=z_s.at[step],
            recv_sem=z_r.at[step],
            device_id={"seq": peer_of(e, step) * span + j},
            device_id_type=MESH,
        )

    def forward(step):
        if step > 0:
            disp(step).wait_recv()
        for d in range(1, span):
            fwd(step, d).start()

    def gate_up(step):
        for d in range(1, span):
            fwd(step, d).wait_recv()

        @pl.loop(0, hidden // ht)
        def _(c):
            for weight, base in ((gate_w, 0), (up_w, hidden)):
                cols = pl.ds(pl.multiple_of(c * ht, ht), ht)
                to = pl.ds(pl.multiple_of(base + c * ht, ht), ht)
                part = jnp.dot(
                    rows_in[step], weight[:, cols], preferred_element_type=jnp.float32
                )
                own_part[step % 2, :, to] = part
                part_send[step, :, to] = part.astype(jnp.bfloat16)

        tp_copy(step).start()

    def down(step):
        tp_copy(step).wait_recv()

        @pl.loop(0, hidden // ht)
        def _(c):
            cols = pl.ds(pl.multiple_of(c * ht, ht), ht)
            ups = pl.ds(pl.multiple_of(hidden + c * ht, ht), ht)
            gate = own_part[step % 2, :, cols] + part_recv[step, :, cols].astype(jnp.float32)
            up = own_part[step % 2, :, ups] + part_recv[step, :, ups].astype(jnp.float32)
            act[:, cols] = (jax.nn.silu(gate) * up).astype(jnp.bfloat16)

        @pl.loop(0, feats // ft)
        def _(c):
            cols = pl.ds(pl.multiple_of(c * ft, ft), ft)
            piece[step, :, cols] = jnp.dot(
                act[...], down_w[:, cols], preferred_element_type=jnp.float32
            ).astype(jnp.bfloat16)

        for d in range(1, span):
            y_copy(step, d).start()

    def give_back(step):
        for d in range(1, span):
            y_copy(step, d).wait_recv()

        @pl.loop(0, feats // ft)
        def _(c):
            cols = pl.ds(pl.multiple_of(c * ft, ft), ft)
            total = piece[step, slots(j), cols].astype(jnp.float32)
            for d in range(1, span):
                total += piece_recv[step, d - 1, :, cols].astype(jnp.float32)
            if step == 0:
                returned[slots(e), cols] = total.astype(jnp.bfloat16)
            else:
                back[step, :, cols] = total.astype(jnp.bfloat16)

        if step > 0:
            z_copy(step).start()

    disp(2).start()
    disp(1).start()
    forward(0)
    rows_in[0, slots(j)] = outgoing[slots(e)]
    weights[0].wait()
    weights[1].wait()
    forward(1)
    gate_up(0)
    disp(3).start()
    forward(2)
    gate_up(1)
    weights[2].wait()
    down(0)
    down(1)
    forward(3)
    gate_up(2)
    give_back(1)
    down(2)
    gate_up(3)
    give_back(2)
    down(3)
    give_back(0)
    give_back(3)
    for step in range(1, experts):
        z_copy(step).wait_recv()

    @pl.loop(0, feats // ft)
    def _(c):
        cols = pl.ds(pl.multiple_of(c * ft, ft), ft)
        picked = jnp.dot(sel_t, returned[:, cols], preferred_element_type=jnp.float32)
        out[:, cols] = (hid[:, cols].astype(jnp.float32) + picked).astype(jnp.bfloat16)

    stat_copy.wait_send()
    for d in range(1, STRETCH_DEVS):

        @pl.when(place + d < STRETCH_DEVS)
        def _():
            kv_copy(keys, key_all, k_s, k_r, d).wait_send()
            kv_copy(values, value_all, v_s, v_r, d).wait_send()

    for step in range(experts):
        if step > 0:
            disp(step).wait_send()
            z_copy(step).wait_send()
        tp_copy(step).wait_send()
        for d in range(1, span):
            fwd(step, d).wait_send()
            y_copy(step, d).wait_send()


def on_device(
    queries,
    key_heads,
    values,
    residual,
    doc_start,
    norm_gain,
    router,
    expert_id,
    slot_index,
    gate_weight,
    up_weight,
    down_weight,
):
    tokens, feats = queries.shape
    hidden = gate_weight.shape[1]
    experts = router.shape[1]
    cap = 3 * tokens // (2 * experts)
    span = lax.axis_size("seq") // experts
    rows = span * cap
    bf16 = jnp.bfloat16
    ids = jnp.stack([doc_start, expert_id, expert_id * cap + slot_index] + [expert_id] * 5)
    vmem = pl.BlockSpec(memory_space=pltpu.VMEM)
    hbm = pl.BlockSpec(memory_space=pl.ANY)
    dma = pltpu.SemaphoreType.DMA
    return pl.pallas_call(
        functools.partial(layer_kernel, span, cap),
        out_shape=jax.ShapeDtypeStruct((tokens, feats), bf16),
        in_specs=[vmem] * 7 + [hbm] * 3,
        out_specs=vmem,
        scratch_shapes=[
            pltpu.VMEM((feats, hidden), bf16),
            pltpu.VMEM((feats, hidden), bf16),
            pltpu.VMEM((hidden, feats), bf16),
            pltpu.VMEM((STRETCH_DEVS, tokens, key_heads.shape[1]), bf16),
            pltpu.VMEM((STRETCH_DEVS, tokens, key_heads.shape[1]), bf16),
            pltpu.VMEM((tokens, STRETCH_DEVS * tokens), jnp.float32),
            pltpu.VMEM((feats // HD, tokens, STRETCH_DEVS * tokens), bf16),
            pltpu.VMEM((feats // HD, tokens, HD), jnp.float32),
            pltpu.VMEM((tokens, feats), bf16),
            pltpu.VMEM((tokens, feats), bf16),
            pltpu.VMEM((tokens, tokens), jnp.float32),
            pltpu.VMEM((tokens, tokens), jnp.float32),
            pltpu.VMEM((experts * cap, feats), bf16),
            pltpu.VMEM((experts, rows, feats), bf16),
            pltpu.VMEM((2, rows, 2 * hidden), jnp.float32),
            pltpu.VMEM((experts, rows, 2 * hidden), bf16),
            pltpu.VMEM((experts, rows, 2 * hidden), bf16),
            pltpu.VMEM((rows, hidden), bf16),
            pltpu.VMEM((experts, rows, feats), bf16),
            pltpu.VMEM((experts, span - 1, cap, feats), bf16),
            pltpu.VMEM((experts, cap, feats), bf16),
            pltpu.VMEM((experts * cap, feats), bf16),
            dma((3,)),
            dma((STRETCH_DEVS,)),
            dma((STRETCH_DEVS,)),
            dma((STRETCH_DEVS,)),
            dma((STRETCH_DEVS,)),
            dma((1,)),
            dma((1,)),
            dma((experts,)),
            dma((experts,)),
            dma((experts, span)),
            dma((experts, span)),
            dma((experts,)),
            dma((experts,)),
            dma((experts, span)),
            dma((experts, span)),
            dma((experts,)),
            dma((experts,)),
        ],
        compiler_params=pltpu.CompilerParams(
            collective_id=0, has_side_effects=True, vmem_limit_bytes=VMEM_LIMIT
        ),
        name="layer",
    )(
        queries,
        key_heads,
        values,
        residual,
        ids,
        norm_gain.reshape(1, feats),
        router,
        gate_weight,
        up_weight,
        down_weight,
    )


def solution(mesh):
    return jax.shard_map(
        on_device,
        mesh=mesh,
        in_specs=(
            P(("grp", "seq"), "tp"),
            P(("grp", "seq"), "tp"),
            P(("grp", "seq"), "tp"),
            P(("grp", "seq"), "tp"),
            P(("grp", "seq")),
            P("tp"),
            P("tp", None),
            P(("grp", "seq")),
            P(("grp", "seq")),
            P("tp", "seq"),
            P("tp", "seq"),
            P("seq", "tp"),
        ),
        out_specs=P(("grp", "seq"), "tp"),
        check_vma=False,
    )
```

```python
import functools
import math

import jax
import jax.numpy as jnp
from jax import lax
from jax.experimental import pallas as pl
from jax.experimental.pallas import tpu as pltpu
from jax.sharding import PartitionSpec as P

D = 5120
QH = 40
KVH = 8
HD = 128
STRETCH_DEVS = 4


MESH = pl.DeviceIdType.MESH
VMEM_LIMIT = 60 * 1024 * 1024


def peer_of(expert, step):
    if step == 0:
        return expert
    if step == 1:
        return expert + 1 - 2 * (expert % 2)
    if step == 2:
        return (expert + 2) % 4
    return 3 - expert


def layer_kernel(
    span,
    cap,
    queries,
    keys,
    values,
    residual,
    starts,
    expert_ids,
    slot_ids,
    gain,
    router,
    gate_hbm,
    up_hbm,
    down_hbm,
    out,
    gate_w,
    up_w,
    down_w,
    key_all,
    value_all,
    bias,
    probs,
    totals,
    hid,
    gained,
    stat,
    stat_recv,
    outgoing,
    rows_in,
    own_part,
    part_send,
    part_recv,
    act,
    piece,
    piece_recv,
    back,
    returned,
    w_sem,
    k_s,
    k_r,
    v_s,
    v_r,
    st_s,
    st_r,
    disp_s,
    disp_r,
    fwd_s,
    fwd_r,
    tp_s,
    tp_r,
    y_s,
    y_r,
    z_s,
    z_r,
):
    experts = 4
    me = lax.axis_index("seq")
    core = lax.axis_index("tp")
    e = me // span
    j = me % span
    feats = queries.shape[1]
    tokens = queries.shape[0]
    hidden = gate_w.shape[1]
    ft = feats // 2
    ht = min(1024, hidden)

    weights = [
        pltpu.make_async_copy(src, dst, w_sem.at[i])
        for i, (src, dst) in enumerate(((gate_hbm, gate_w), (up_hbm, up_w), (down_hbm, down_w)))
    ]
    for copy in weights:
        copy.start()

    barrier = pltpu.get_barrier_semaphore()
    for step in range(1, experts):
        pl.semaphore_signal(
            barrier, inc=1, device_id={"seq": peer_of(e, step) * span + j}, device_id_type=MESH
        )
    for d in range(1, span):
        pl.semaphore_signal(
            barrier, inc=1, device_id={"seq": e * span + (j + d) % span}, device_id_type=MESH
        )
    pl.semaphore_signal(barrier, inc=1, device_id={"tp": 1 - core}, device_id_type=MESH)
    place = me % STRETCH_DEVS
    for d in range(1, STRETCH_DEVS):
        pl.semaphore_signal(
            barrier,
            inc=1,
            device_id={"seq": me - place + (place + d) % STRETCH_DEVS},
            device_id_type=MESH,
        )

    def slots(number):
        return pl.ds(pl.multiple_of(number * cap, 16), cap)

    f32 = jnp.float32
    key_all[0] = keys[...]
    value_all[0] = values[...]

    across = lax.broadcasted_iota(jnp.int32, (tokens, tokens), 1)
    below = lax.broadcasted_iota(jnp.int32, (tokens, tokens), 0)

    def column(row):
        spread = jnp.broadcast_to(row.astype(f32), (tokens, tokens))
        return jnp.sum(jnp.where(across == below, spread, 0.0), axis=1, keepdims=True).astype(
            jnp.int32
        )

    place_row = expert_ids[...] * cap + slot_ids[...]
    start_col = column(starts[...])
    expert_col = column(expert_ids[...])
    place_col = column(place_row)
    query_pos = me * tokens + below
    for d in range(STRETCH_DEVS):
        key_pos = (me - d) * tokens + across
        allowed = (
            (key_pos <= query_pos) & (key_pos >= start_col) & (key_pos >= (me - place) * tokens)
        )
        bias[:, d * tokens : (d + 1) * tokens] = jnp.where(allowed, 0.0, -jnp.inf)

    pl.semaphore_wait(barrier, experts - 1 + span + STRETCH_DEVS - 1)

    def kv_copy(src, dst, send, recv, d):
        return pltpu.make_async_remote_copy(
            src_ref=src,
            dst_ref=dst.at[d],
            send_sem=send.at[d],
            recv_sem=recv.at[d],
            device_id={"seq": me + d},
            device_id_type=MESH,
        )

    for src, dst, send, recv in (
        (keys, key_all, k_s, k_r),
        (values, value_all, v_s, v_r),
    ):
        for d in range(STRETCH_DEVS - 1, 0, -1):

            @pl.when(place + d < STRETCH_DEVS)
            def _():
                kv_copy(src, dst, send, recv, d).start()

            @pl.when(place < d)
            def _():
                dst[d] = jnp.zeros_like(src)

    for d in range(1, STRETCH_DEVS):

        @pl.when(place >= d)
        def _():
            kv_copy(keys, key_all, k_s, k_r, d).wait_recv()

    kv_heads = keys.shape[1] // HD
    per_group = QH // KVH
    scale = math.log2(math.e) / math.sqrt(HD)

    @pl.loop(0, kv_heads)
    def _(g):
        kcols = pl.ds(pl.multiple_of(g * HD, HD), HD)
        key_block = key_all[:, :, kcols].reshape(STRETCH_DEVS * tokens, HD)
        for r in range(per_group):
            h = g * per_group + r
            cols = pl.ds(pl.multiple_of(h * HD, HD), HD)
            scores = lax.dot_general(
                queries[:, cols], key_block, (((1,), (1,)), ((), ())), preferred_element_type=f32
            )
            masked = scores + bias[...]
            largest = jnp.max(masked, axis=1, keepdims=True)
            expo = jnp.exp2((masked - largest) * scale)
            totals[h] = jnp.broadcast_to(jnp.sum(expo, axis=1, keepdims=True), (tokens, HD))
            probs[h] = expo.astype(jnp.bfloat16)

    for d in range(1, STRETCH_DEVS):

        @pl.when(place >= d)
        def _():
            kv_copy(values, value_all, v_s, v_r, d).wait_recv()

    stat[...] = jnp.zeros_like(stat)

    @pl.loop(0, kv_heads)
    def _(g):
        kcols = pl.ds(pl.multiple_of(g * HD, HD), HD)
        value_block = value_all[:, :, kcols].reshape(STRETCH_DEVS * tokens, HD)
        for r in range(per_group):
            h = g * per_group + r
            cols = pl.ds(pl.multiple_of(h * HD, HD), HD)
            attended = jnp.dot(probs[h], value_block, preferred_element_type=f32) / totals[h]
            state = (residual[:, cols].astype(f32) + attended).astype(jnp.bfloat16)
            hid[:, cols] = state
            wide = state.astype(f32)
            gained[:, cols] = (wide * gain[:, cols].astype(f32)).astype(jnp.bfloat16)
            stat[...] += wide * wide

    square = jnp.sum(stat[...], axis=1, keepdims=True)
    logits = lax.dot_general(
        gained[...], router[...], (((1,), (1,)), ((), ())), preferred_element_type=f32
    )
    lane = lax.broadcasted_iota(jnp.int32, (tokens, experts), 1)
    picked = jnp.sum(jnp.where(lane == expert_col, logits, 0.0), axis=1, keepdims=True)
    stat[...] = jnp.where(across == 0, picked, square)
    stat_copy = pltpu.make_async_remote_copy(
        src_ref=stat,
        dst_ref=stat_recv,
        send_sem=st_s.at[0],
        recv_sem=st_r.at[0],
        device_id={"tp": 1 - core},
        device_id_type=MESH,
    )
    stat_copy.start()
    slot_row = lax.broadcasted_iota(jnp.int32, (experts * cap, tokens), 0)
    slot_lane = lax.broadcasted_iota(jnp.int32, (tokens, experts * cap), 1)
    sel = jnp.where(slot_row == place_row, 1.0, 0.0).astype(jnp.bfloat16)
    sel_t = jnp.where(slot_lane == place_col, 1.0, 0.0).astype(jnp.bfloat16)
    stat_copy.wait_recv()
    both = stat[...] + stat_recv[...]
    inverse = lax.rsqrt(both[:, 1:2] / D + 1e-05)
    factor = inverse * jax.nn.sigmoid(inverse * both[:, 0:1])

    @pl.loop(0, feats // ft)
    def _(c):
        cols = pl.ds(pl.multiple_of(c * ft, ft), ft)
        expert_in = (gained[:, cols].astype(f32) * factor).astype(jnp.bfloat16)
        outgoing[:, cols] = jnp.dot(sel, expert_in, preferred_element_type=f32).astype(
            jnp.bfloat16
        )

    edge = feats // (2 * ft) * ft + (ft if feats % (2 * ft) else 0)
    halves = ((0, edge), (edge, feats - edge))

    def half(part):
        return pl.ds(*halves[part])

    def disp(step, part):
        return pltpu.make_async_remote_copy(
            src_ref=outgoing.at[slots(peer_of(e, step)), half(part)],
            dst_ref=rows_in.at[step, slots(j), half(part)],
            send_sem=disp_s.at[step, part],
            recv_sem=disp_r.at[step, part],
            device_id={"seq": peer_of(e, step) * span + j},
            device_id_type=MESH,
        )

    def fwd(step, d, part):
        if step == 0:
            src = outgoing.at[slots(e), half(part)]
        else:
            src = rows_in.at[step, slots(j), half(part)]
        return pltpu.make_async_remote_copy(
            src_ref=src,
            dst_ref=rows_in.at[step, slots(j), half(part)],
            send_sem=fwd_s.at[step, d, part],
            recv_sem=fwd_r.at[step, d, part],
            device_id={"seq": e * span + (j + d) % span},
            device_id_type=MESH,
        )

    def tp_copy(step):
        return pltpu.make_async_remote_copy(
            src_ref=part_send.at[step],
            dst_ref=part_recv.at[step],
            send_sem=tp_s.at[step],
            recv_sem=tp_r.at[step],
            device_id={"tp": 1 - core},
            device_id_type=MESH,
        )

    def y_copy(step, d, part):
        return pltpu.make_async_remote_copy(
            src_ref=piece.at[step, slots((j + d) % span), half(part)],
            dst_ref=piece_recv.at[step, d - 1, :, half(part)],
            send_sem=y_s.at[step, d, part],
            recv_sem=y_r.at[step, d, part],
            device_id={"seq": e * span + (j + d) % span},
            device_id_type=MESH,
        )

    def z_copy(step, part):
        return pltpu.make_async_remote_copy(
            src_ref=back.at[step, :, half(part)],
            dst_ref=returned.at[slots(e), half(part)],
            send_sem=z_s.at[step, part],
            recv_sem=z_r.at[step, part],
            device_id={"seq": peer_of(e, step) * span + j},
            device_id_type=MESH,
        )

    def dispatch(step):
        for part in range(2):
            disp(step, part).start()

    def forward(step):
        for part in range(2):
            if step > 0:
                disp(step, part).wait_recv()
            for d in range(1, span):
                fwd(step, d, part).start()

    def arrived(step):
        for part in range(2):
            for d in range(1, span):
                fwd(step, d, part).wait_recv()

    def gate_up(step):
        @pl.loop(0, hidden // ht)
        def _(c):
            for weight, base in ((gate_w, 0), (up_w, hidden)):
                cols = pl.ds(pl.multiple_of(c * ht, ht), ht)
                to = pl.ds(pl.multiple_of(base + c * ht, ht), ht)
                part = jnp.dot(
                    rows_in[step], weight[:, cols], preferred_element_type=jnp.float32
                )
                own_part[step % 2, :, to] = part
                part_send[step, :, to] = part.astype(jnp.bfloat16)

        tp_copy(step).start()

    def down(step):
        tp_copy(step).wait_recv()

        @pl.loop(0, hidden // ht)
        def _(c):
            cols = pl.ds(pl.multiple_of(c * ht, ht), ht)
            ups = pl.ds(pl.multiple_of(hidden + c * ht, ht), ht)
            gate = own_part[step % 2, :, cols] + part_recv[step, :, cols].astype(jnp.float32)
            up = own_part[step % 2, :, ups] + part_recv[step, :, ups].astype(jnp.float32)
            act[:, cols] = (jax.nn.silu(gate) * up).astype(jnp.bfloat16)

        for part, (low, size) in enumerate(halves):

            @pl.loop(low // ft, (low + size) // ft)
            def _(c):
                cols = pl.ds(pl.multiple_of(c * ft, ft), ft)
                piece[step, :, cols] = jnp.dot(
                    act[...], down_w[:, cols], preferred_element_type=jnp.float32
                ).astype(jnp.bfloat16)

            for d in range(1, span):
                y_copy(step, d, part).start()

    def give_back(step):
        for part, (low, size) in enumerate(halves):
            for d in range(1, span):
                y_copy(step, d, part).wait_recv()

            @pl.loop(low // ft, (low + size) // ft)
            def _(c):
                cols = pl.ds(pl.multiple_of(c * ft, ft), ft)
                total = piece[step, slots(j), cols].astype(jnp.float32)
                for d in range(1, span):
                    total += piece_recv[step, d - 1, :, cols].astype(jnp.float32)
                if step == 0:
                    returned[slots(e), cols] = total.astype(jnp.bfloat16)
                else:
                    back[step, :, cols] = total.astype(jnp.bfloat16)

            if step > 0:
                z_copy(step, part).start()

    dispatch(2)
    forward(0)
    rows_in[0, slots(j)] = outgoing[slots(e)]
    weights[0].wait()
    weights[1].wait()
    arrived(0)
    gate_up(0)
    dispatch(3)
    dispatch(1)
    forward(2)
    weights[2].wait()
    arrived(2)
    down(0)
    gate_up(2)
    forward(1)
    forward(3)
    down(2)
    arrived(1)
    gate_up(1)
    give_back(2)
    arrived(3)
    down(1)
    gate_up(3)
    give_back(1)
    down(3)
    give_back(0)
    give_back(3)
    for part, (low, size) in enumerate(halves):
        for step in range(1, experts):
            z_copy(step, part).wait_recv()

        @pl.loop(low // ft, (low + size) // ft)
        def _(c):
            cols = pl.ds(pl.multiple_of(c * ft, ft), ft)
            picked = jnp.dot(sel_t, returned[:, cols], preferred_element_type=jnp.float32)
            out[:, cols] = (hid[:, cols].astype(jnp.float32) + picked).astype(jnp.bfloat16)

    stat_copy.wait_send()
    for d in range(1, STRETCH_DEVS):

        @pl.when(place + d < STRETCH_DEVS)
        def _():
            kv_copy(keys, key_all, k_s, k_r, d).wait_send()
            kv_copy(values, value_all, v_s, v_r, d).wait_send()

    for step in range(experts):
        tp_copy(step).wait_send()
        for part in range(2):
            if step > 0:
                disp(step, part).wait_send()
                z_copy(step, part).wait_send()
            for d in range(1, span):
                fwd(step, d, part).wait_send()
                y_copy(step, d, part).wait_send()


def on_device(
    queries,
    key_heads,
    values,
    residual,
    doc_start,
    norm_gain,
    router,
    expert_id,
    slot_index,
    gate_weight,
    up_weight,
    down_weight,
):
    tokens, feats = queries.shape
    hidden = gate_weight.shape[1]
    experts = router.shape[1]
    cap = 3 * tokens // (2 * experts)
    span = lax.axis_size("seq") // experts
    rows = span * cap
    bf16 = jnp.bfloat16
    vmem = pl.BlockSpec(memory_space=pltpu.VMEM)
    hbm = pl.BlockSpec(memory_space=pl.ANY)
    dma = pltpu.SemaphoreType.DMA
    return pl.pallas_call(
        functools.partial(layer_kernel, span, cap),
        out_shape=jax.ShapeDtypeStruct((tokens, feats), bf16),
        in_specs=[vmem] * 9 + [hbm] * 3,
        out_specs=vmem,
        scratch_shapes=[
            pltpu.VMEM((feats, hidden), bf16),
            pltpu.VMEM((feats, hidden), bf16),
            pltpu.VMEM((hidden, feats), bf16),
            pltpu.VMEM((STRETCH_DEVS, tokens, key_heads.shape[1]), bf16),
            pltpu.VMEM((STRETCH_DEVS, tokens, key_heads.shape[1]), bf16),
            pltpu.VMEM((tokens, STRETCH_DEVS * tokens), jnp.float32),
            pltpu.VMEM((feats // HD, tokens, STRETCH_DEVS * tokens), bf16),
            pltpu.VMEM((feats // HD, tokens, HD), jnp.float32),
            pltpu.VMEM((tokens, feats), bf16),
            pltpu.VMEM((tokens, feats), bf16),
            pltpu.VMEM((tokens, tokens), jnp.float32),
            pltpu.VMEM((tokens, tokens), jnp.float32),
            pltpu.VMEM((experts * cap, feats), bf16),
            pltpu.VMEM((experts, rows, feats), bf16),
            pltpu.VMEM((2, rows, 2 * hidden), jnp.float32),
            pltpu.VMEM((experts, rows, 2 * hidden), bf16),
            pltpu.VMEM((experts, rows, 2 * hidden), bf16),
            pltpu.VMEM((rows, hidden), bf16),
            pltpu.VMEM((experts, rows, feats), bf16),
            pltpu.VMEM((experts, span - 1, cap, feats), bf16),
            pltpu.VMEM((experts, cap, feats), bf16),
            pltpu.VMEM((experts * cap, feats), bf16),
            dma((3,)),
            dma((STRETCH_DEVS,)),
            dma((STRETCH_DEVS,)),
            dma((STRETCH_DEVS,)),
            dma((STRETCH_DEVS,)),
            dma((1,)),
            dma((1,)),
            dma((experts, 2)),
            dma((experts, 2)),
            dma((experts, span, 2)),
            dma((experts, span, 2)),
            dma((experts,)),
            dma((experts,)),
            dma((experts, span, 2)),
            dma((experts, span, 2)),
            dma((experts, 2)),
            dma((experts, 2)),
        ],
        compiler_params=pltpu.CompilerParams(
            collective_id=0, has_side_effects=True, vmem_limit_bytes=VMEM_LIMIT
        ),
        name="layer",
    )(
        queries,
        key_heads,
        values,
        residual,
        doc_start.reshape(1, tokens),
        expert_id.reshape(1, tokens),
        slot_index.reshape(1, tokens),
        norm_gain.reshape(1, feats),
        router.T,
        gate_weight,
        up_weight,
        down_weight,
    )


def solution(mesh):
    return jax.shard_map(
        on_device,
        mesh=mesh,
        in_specs=(
            P(("grp", "seq"), "tp"),
            P(("grp", "seq"), "tp"),
            P(("grp", "seq"), "tp"),
            P(("grp", "seq"), "tp"),
            P(("grp", "seq")),
            P("tp"),
            P("tp", None),
            P(("grp", "seq")),
            P(("grp", "seq")),
            P("tp", "seq"),
            P("tp", "seq"),
            P("seq", "tp"),
        ),
        out_specs=P(("grp", "seq"), "tp"),
        check_vma=False,
    )
```

```python
import functools
import math

import jax
import jax.numpy as jnp
from jax import lax
from jax.experimental import pallas as pl
from jax.experimental.pallas import tpu as pltpu
from jax.sharding import PartitionSpec as P

D = 5120
QH = 40
KVH = 8
HD = 128
STRETCH_DEVS = 4


MESH = pl.DeviceIdType.MESH
VMEM_LIMIT = 60 * 1024 * 1024


def peer_of(expert, step):
    if step == 0:
        return expert
    if step == 1:
        return expert + 1 - 2 * (expert % 2)
    if step == 2:
        return (expert + 2) % 4
    return 3 - expert


def layer_kernel(
    span,
    cap,
    queries,
    keys,
    values,
    residual,
    starts,
    expert_ids,
    slot_ids,
    gain,
    router,
    gate_hbm,
    up_hbm,
    down_hbm,
    out,
    gate_w,
    up_w,
    down_w,
    key_all,
    value_all,
    bias,
    probs,
    totals,
    hid,
    gained,
    stat,
    stat_recv,
    outgoing,
    rows_in,
    own_part,
    part_send,
    part_recv,
    act,
    piece,
    piece_recv,
    back,
    returned,
    w_sem,
    k_s,
    k_r,
    v_s,
    v_r,
    st_s,
    st_r,
    disp_s,
    disp_r,
    fwd_s,
    fwd_r,
    tp_s,
    tp_r,
    y_s,
    y_r,
    z_s,
    z_r,
):
    experts = 4
    me = lax.axis_index("seq")
    core = lax.axis_index("tp")
    e = me // span
    j = me % span
    feats = queries.shape[1]
    tokens = queries.shape[0]
    hidden = gate_w.shape[1]
    ft = feats // 2
    ht = min(1024, hidden)

    weights = [
        pltpu.make_async_copy(src, dst, w_sem.at[i])
        for i, (src, dst) in enumerate(((gate_hbm, gate_w), (up_hbm, up_w), (down_hbm, down_w)))
    ]
    for copy in weights:
        copy.start()

    barrier = pltpu.get_barrier_semaphore()
    for step in range(1, experts):
        pl.semaphore_signal(
            barrier, inc=1, device_id={"seq": peer_of(e, step) * span + j}, device_id_type=MESH
        )
    for d in range(1, span):
        pl.semaphore_signal(
            barrier, inc=1, device_id={"seq": e * span + (j + d) % span}, device_id_type=MESH
        )
    pl.semaphore_signal(barrier, inc=1, device_id={"tp": 1 - core}, device_id_type=MESH)
    place = me % STRETCH_DEVS
    for d in range(1, STRETCH_DEVS):
        pl.semaphore_signal(
            barrier,
            inc=1,
            device_id={"seq": me - place + (place + d) % STRETCH_DEVS},
            device_id_type=MESH,
        )

    def slots(number):
        return pl.ds(pl.multiple_of(number * cap, 16), cap)

    f32 = jnp.float32
    key_all[0] = keys[...]
    value_all[0] = values[...]

    across = lax.broadcasted_iota(jnp.int32, (tokens, tokens), 1)
    below = lax.broadcasted_iota(jnp.int32, (tokens, tokens), 0)

    def column(row):
        spread = jnp.broadcast_to(row.astype(f32), (tokens, tokens))
        return jnp.sum(jnp.where(across == below, spread, 0.0), axis=1, keepdims=True).astype(
            jnp.int32
        )

    place_row = expert_ids[...] * cap + slot_ids[...]
    start_col = column(starts[...])
    expert_col = column(expert_ids[...])
    place_col = column(place_row)
    query_pos = me * tokens + below
    for d in range(STRETCH_DEVS):
        key_pos = (me - d) * tokens + across
        allowed = (
            (key_pos <= query_pos) & (key_pos >= start_col) & (key_pos >= (me - place) * tokens)
        )
        bias[:, d * tokens : (d + 1) * tokens] = jnp.where(allowed, 0.0, -jnp.inf)

    pl.semaphore_wait(barrier, experts - 1 + span + STRETCH_DEVS - 1)

    def kv_copy(src, dst, send, recv, d):
        return pltpu.make_async_remote_copy(
            src_ref=src,
            dst_ref=dst.at[d],
            send_sem=send.at[d],
            recv_sem=recv.at[d],
            device_id={"seq": me + d},
            device_id_type=MESH,
        )

    def send_on(src, dst, send, recv):
        for d in range(STRETCH_DEVS - 1, 0, -1):

            @pl.when(place + d < STRETCH_DEVS)
            def _():
                kv_copy(src, dst, send, recv, d).start()

            @pl.when(place < d)
            def _():
                dst[d] = jnp.zeros_like(src)

    send_on(keys, key_all, k_s, k_r)
    for d in range(1, STRETCH_DEVS):

        @pl.when(place + d < STRETCH_DEVS)
        def _():
            kv_copy(keys, key_all, k_s, k_r, d).wait_send()

    send_on(values, value_all, v_s, v_r)

    for d in range(1, STRETCH_DEVS):

        @pl.when(place >= d)
        def _():
            kv_copy(keys, key_all, k_s, k_r, d).wait_recv()

    kv_heads = keys.shape[1] // HD
    per_group = QH // KVH
    scale = math.log2(math.e) / math.sqrt(HD)

    @pl.loop(0, kv_heads)
    def _(g):
        kcols = pl.ds(pl.multiple_of(g * HD, HD), HD)
        key_block = key_all[:, :, kcols].reshape(STRETCH_DEVS * tokens, HD)
        for r in range(per_group):
            h = g * per_group + r
            cols = pl.ds(pl.multiple_of(h * HD, HD), HD)
            scores = lax.dot_general(
                queries[:, cols], key_block, (((1,), (1,)), ((), ())), preferred_element_type=f32
            )
            masked = scores + bias[...]
            largest = jnp.max(masked, axis=1, keepdims=True)
            expo = jnp.exp2((masked - largest) * scale)
            totals[h] = jnp.broadcast_to(jnp.sum(expo, axis=1, keepdims=True), (tokens, HD))
            probs[h] = expo.astype(jnp.bfloat16)

    for d in range(1, STRETCH_DEVS):

        @pl.when(place >= d)
        def _():
            kv_copy(values, value_all, v_s, v_r, d).wait_recv()

    stat[...] = jnp.zeros_like(stat)

    @pl.loop(0, kv_heads)
    def _(g):
        kcols = pl.ds(pl.multiple_of(g * HD, HD), HD)
        value_block = value_all[:, :, kcols].reshape(STRETCH_DEVS * tokens, HD)
        for r in range(per_group):
            h = g * per_group + r
            cols = pl.ds(pl.multiple_of(h * HD, HD), HD)
            attended = jnp.dot(probs[h], value_block, preferred_element_type=f32) / totals[h]
            state = (residual[:, cols].astype(f32) + attended).astype(jnp.bfloat16)
            hid[:, cols] = state
            wide = state.astype(f32)
            gained[:, cols] = (wide * gain[:, cols].astype(f32)).astype(jnp.bfloat16)
            stat[...] += wide * wide

    square = jnp.sum(stat[...], axis=1, keepdims=True)
    logits = lax.dot_general(
        gained[...], router[...], (((1,), (1,)), ((), ())), preferred_element_type=f32
    )
    lane = lax.broadcasted_iota(jnp.int32, (tokens, experts), 1)
    picked = jnp.sum(jnp.where(lane == expert_col, logits, 0.0), axis=1, keepdims=True)
    stat[...] = jnp.where(across == 0, picked, square)
    stat_copy = pltpu.make_async_remote_copy(
        src_ref=stat,
        dst_ref=stat_recv,
        send_sem=st_s.at[0],
        recv_sem=st_r.at[0],
        device_id={"tp": 1 - core},
        device_id_type=MESH,
    )
    stat_copy.start()
    slot_row = lax.broadcasted_iota(jnp.int32, (experts * cap, tokens), 0)
    slot_lane = lax.broadcasted_iota(jnp.int32, (tokens, experts * cap), 1)
    sel = jnp.where(slot_row == place_row, 1.0, 0.0).astype(jnp.bfloat16)
    sel_t = jnp.where(slot_lane == place_col, 1.0, 0.0).astype(jnp.bfloat16)
    stat_copy.wait_recv()
    both = stat[...] + stat_recv[...]
    inverse = lax.rsqrt(both[:, 1:2] / D + 1e-05)
    factor = inverse * jax.nn.sigmoid(inverse * both[:, 0:1])

    @pl.loop(0, feats // ft)
    def _(c):
        cols = pl.ds(pl.multiple_of(c * ft, ft), ft)
        expert_in = (gained[:, cols].astype(f32) * factor).astype(jnp.bfloat16)
        outgoing[:, cols] = jnp.dot(sel, expert_in, preferred_element_type=f32).astype(
            jnp.bfloat16
        )

    edge = feats // (2 * ft) * ft + (ft if feats % (2 * ft) else 0)
    halves = ((0, edge), (edge, feats - edge))

    def half(part):
        return pl.ds(*halves[part])

    def disp(step, part):
        return pltpu.make_async_remote_copy(
            src_ref=outgoing.at[slots(peer_of(e, step)), half(part)],
            dst_ref=rows_in.at[step, slots(j), half(part)],
            send_sem=disp_s.at[step, part],
            recv_sem=disp_r.at[step, part],
            device_id={"seq": peer_of(e, step) * span + j},
            device_id_type=MESH,
        )

    def fwd(step, d, part):
        if step == 0:
            src = outgoing.at[slots(e), half(part)]
        else:
            src = rows_in.at[step, slots(j), half(part)]
        return pltpu.make_async_remote_copy(
            src_ref=src,
            dst_ref=rows_in.at[step, slots(j), half(part)],
            send_sem=fwd_s.at[step, d, part],
            recv_sem=fwd_r.at[step, d, part],
            device_id={"seq": e * span + (j + d) % span},
            device_id_type=MESH,
        )

    def tp_copy(step):
        return pltpu.make_async_remote_copy(
            src_ref=part_send.at[step],
            dst_ref=part_recv.at[step],
            send_sem=tp_s.at[step],
            recv_sem=tp_r.at[step],
            device_id={"tp": 1 - core},
            device_id_type=MESH,
        )

    def y_copy(step, d, part):
        return pltpu.make_async_remote_copy(
            src_ref=piece.at[step, slots((j + d) % span), half(part)],
            dst_ref=piece_recv.at[step, d - 1, :, half(part)],
            send_sem=y_s.at[step, d, part],
            recv_sem=y_r.at[step, d, part],
            device_id={"seq": e * span + (j + d) % span},
            device_id_type=MESH,
        )

    def z_copy(step, part):
        return pltpu.make_async_remote_copy(
            src_ref=back.at[step, :, half(part)],
            dst_ref=returned.at[slots(e), half(part)],
            send_sem=z_s.at[step, part],
            recv_sem=z_r.at[step, part],
            device_id={"seq": peer_of(e, step) * span + j},
            device_id_type=MESH,
        )

    def dispatch(step):
        for part in range(2):
            disp(step, part).start()

    def forward(step):
        for part in range(2):
            if step > 0:
                disp(step, part).wait_recv()
            for d in range(1, span):
                fwd(step, d, part).start()

    def arrived(step):
        for part in range(2):
            for d in range(1, span):
                fwd(step, d, part).wait_recv()

    def gate_up(step):
        @pl.loop(0, hidden // ht)
        def _(c):
            for weight, base in ((gate_w, 0), (up_w, hidden)):
                cols = pl.ds(pl.multiple_of(c * ht, ht), ht)
                to = pl.ds(pl.multiple_of(base + c * ht, ht), ht)
                part = jnp.dot(
                    rows_in[step], weight[:, cols], preferred_element_type=jnp.float32
                )
                own_part[step % 2, :, to] = part
                part_send[step, :, to] = part.astype(jnp.bfloat16)

        tp_copy(step).start()

    def down(step):
        tp_copy(step).wait_recv()

        @pl.loop(0, hidden // ht)
        def _(c):
            cols = pl.ds(pl.multiple_of(c * ht, ht), ht)
            ups = pl.ds(pl.multiple_of(hidden + c * ht, ht), ht)
            gate = own_part[step % 2, :, cols] + part_recv[step, :, cols].astype(jnp.float32)
            up = own_part[step % 2, :, ups] + part_recv[step, :, ups].astype(jnp.float32)
            act[:, cols] = (jax.nn.silu(gate) * up).astype(jnp.bfloat16)

        for part, (low, size) in enumerate(halves):

            @pl.loop(low // ft, (low + size) // ft)
            def _(c):
                cols = pl.ds(pl.multiple_of(c * ft, ft), ft)
                piece[step, :, cols] = jnp.dot(
                    act[...], down_w[:, cols], preferred_element_type=jnp.float32
                ).astype(jnp.bfloat16)

            for d in range(1, span):
                y_copy(step, d, part).start()

    def give_back(step):
        for part, (low, size) in enumerate(halves):
            for d in range(1, span):
                y_copy(step, d, part).wait_recv()

            @pl.loop(low // ft, (low + size) // ft)
            def _(c):
                cols = pl.ds(pl.multiple_of(c * ft, ft), ft)
                total = piece[step, slots(j), cols].astype(jnp.float32)
                for d in range(1, span):
                    total += piece_recv[step, d - 1, :, cols].astype(jnp.float32)
                if step == 0:
                    returned[slots(e), cols] = total.astype(jnp.bfloat16)
                else:
                    back[step, :, cols] = total.astype(jnp.bfloat16)

            if step > 0:
                z_copy(step, part).start()

    dispatch(2)
    forward(0)
    rows_in[0, slots(j)] = outgoing[slots(e)]
    weights[0].wait()
    weights[1].wait()
    arrived(0)
    gate_up(0)
    dispatch(3)
    dispatch(1)
    forward(2)
    weights[2].wait()
    arrived(2)
    down(0)
    gate_up(2)
    forward(1)
    forward(3)
    down(2)
    arrived(1)
    gate_up(1)
    give_back(2)
    arrived(3)
    down(1)
    gate_up(3)
    give_back(1)
    down(3)
    give_back(0)
    give_back(3)
    for part, (low, size) in enumerate(halves):
        for step in range(1, experts):
            z_copy(step, part).wait_recv()

        @pl.loop(low // ft, (low + size) // ft)
        def _(c):
            cols = pl.ds(pl.multiple_of(c * ft, ft), ft)
            picked = jnp.dot(sel_t, returned[:, cols], preferred_element_type=jnp.float32)
            out[:, cols] = (hid[:, cols].astype(jnp.float32) + picked).astype(jnp.bfloat16)

    stat_copy.wait_send()
    for d in range(1, STRETCH_DEVS):

        @pl.when(place + d < STRETCH_DEVS)
        def _():
            kv_copy(values, value_all, v_s, v_r, d).wait_send()

    for step in range(experts):
        tp_copy(step).wait_send()
        for part in range(2):
            if step > 0:
                disp(step, part).wait_send()
                z_copy(step, part).wait_send()
            for d in range(1, span):
                fwd(step, d, part).wait_send()
                y_copy(step, d, part).wait_send()


def on_device(
    queries,
    key_heads,
    values,
    residual,
    doc_start,
    norm_gain,
    router,
    expert_id,
    slot_index,
    gate_weight,
    up_weight,
    down_weight,
):
    tokens, feats = queries.shape
    hidden = gate_weight.shape[1]
    experts = router.shape[1]
    cap = 3 * tokens // (2 * experts)
    span = lax.axis_size("seq") // experts
    rows = span * cap
    bf16 = jnp.bfloat16
    vmem = pl.BlockSpec(memory_space=pltpu.VMEM)
    hbm = pl.BlockSpec(memory_space=pl.ANY)
    dma = pltpu.SemaphoreType.DMA
    return pl.pallas_call(
        functools.partial(layer_kernel, span, cap),
        out_shape=jax.ShapeDtypeStruct((tokens, feats), bf16),
        in_specs=[vmem] * 9 + [hbm] * 3,
        out_specs=vmem,
        scratch_shapes=[
            pltpu.VMEM((feats, hidden), bf16),
            pltpu.VMEM((feats, hidden), bf16),
            pltpu.VMEM((hidden, feats), bf16),
            pltpu.VMEM((STRETCH_DEVS, tokens, key_heads.shape[1]), bf16),
            pltpu.VMEM((STRETCH_DEVS, tokens, key_heads.shape[1]), bf16),
            pltpu.VMEM((tokens, STRETCH_DEVS * tokens), jnp.float32),
            pltpu.VMEM((feats // HD, tokens, STRETCH_DEVS * tokens), bf16),
            pltpu.VMEM((feats // HD, tokens, HD), jnp.float32),
            pltpu.VMEM((tokens, feats), bf16),
            pltpu.VMEM((tokens, feats), bf16),
            pltpu.VMEM((tokens, tokens), jnp.float32),
            pltpu.VMEM((tokens, tokens), jnp.float32),
            pltpu.VMEM((experts * cap, feats), bf16),
            pltpu.VMEM((experts, rows, feats), bf16),
            pltpu.VMEM((2, rows, 2 * hidden), jnp.float32),
            pltpu.VMEM((experts, rows, 2 * hidden), bf16),
            pltpu.VMEM((experts, rows, 2 * hidden), bf16),
            pltpu.VMEM((rows, hidden), bf16),
            pltpu.VMEM((experts, rows, feats), bf16),
            pltpu.VMEM((experts, span - 1, cap, feats), bf16),
            pltpu.VMEM((experts, cap, feats), bf16),
            pltpu.VMEM((experts * cap, feats), bf16),
            dma((3,)),
            dma((STRETCH_DEVS,)),
            dma((STRETCH_DEVS,)),
            dma((STRETCH_DEVS,)),
            dma((STRETCH_DEVS,)),
            dma((1,)),
            dma((1,)),
            dma((experts, 2)),
            dma((experts, 2)),
            dma((experts, span, 2)),
            dma((experts, span, 2)),
            dma((experts,)),
            dma((experts,)),
            dma((experts, span, 2)),
            dma((experts, span, 2)),
            dma((experts, 2)),
            dma((experts, 2)),
        ],
        compiler_params=pltpu.CompilerParams(
            collective_id=0, has_side_effects=True, vmem_limit_bytes=VMEM_LIMIT
        ),
        name="layer",
    )(
        queries,
        key_heads,
        values,
        residual,
        doc_start.reshape(1, tokens),
        expert_id.reshape(1, tokens),
        slot_index.reshape(1, tokens),
        norm_gain.reshape(1, feats),
        router.T,
        gate_weight,
        up_weight,
        down_weight,
    )


def solution(mesh):
    return jax.shard_map(
        on_device,
        mesh=mesh,
        in_specs=(
            P(("grp", "seq"), "tp"),
            P(("grp", "seq"), "tp"),
            P(("grp", "seq"), "tp"),
            P(("grp", "seq"), "tp"),
            P(("grp", "seq")),
            P("tp"),
            P("tp", None),
            P(("grp", "seq")),
            P(("grp", "seq")),
            P("tp", "seq"),
            P("tp", "seq"),
            P("seq", "tp"),
        ),
        out_specs=P(("grp", "seq"), "tp"),
        check_vma=False,
    )
```
